32 devices in a mesh: blk: 16 (over z, x, core), rep: 2 (over y).
Axes of the slice: x: 2, y: 2, z: 4, core: 2. Of those that a mesh axis runs over, the one named last changes fastest.
Arguments:
- integrals: bfloat16 [16, 512, 1024], P('blk'), may hold values from -0.59765625 to 0.59765625
- eps_occ: float32 [16], replicated, may hold values from -2 to -0.5
- eps_vir: float32 [512], replicated, may hold values from 0.5 to 3
- offsets: int32 [8], P('rep'), may hold values from 0 to 7
Outputs:
- gamma: float32 [16, 512, 1024], P('blk', None, 'rep')
The draws below stay inside these ranges and needn't reach their ends.
All inputs are finite; a program needn't handle non-finite values.
Results may differ from the reference program's by a relative error of at most 0.0017.
Values may be sent and summed in bfloat16 or wider, within the bound.
No kernel may reach another device: no remote copies, remote signals or barrier semaphores. Data moves between devices by JAX's collectives and lax.ppermute only.
A program may use at most 64 MiB of HBM per device.

```python
import jax
import jax.numpy as jnp
from jax import lax

V = 512
AUX = 1024
OCC = 16
PAIRS = 8


def with_ends(array, key, smallest, largest):
    longest = array.shape.index(max(array.shape))
    spots = []
    for shift in (0, 1):
        where = [jax.random.randint(jax.random.fold_in(key, axis), (), 0, length) for axis, length in enumerate(array.shape)]
        where[longest] = (where[longest] + shift) % array.shape[longest]
        spots.append(tuple(where))
    return array.at[spots[0]].set(smallest).at[spots[1]].set(largest)


def level_of(stream_key, dims, cuts, smallest, top_value):
    gain, own = 1.0, jax.random.fold_in(stream_key, 6)
    for dim, blocks in cuts:
        heights = jnp.exp(jax.random.uniform(jax.random.fold_in(own, dim), (blocks,), jnp.float32, smallest / len(cuts), top_value / len(cuts)))
        gain = gain * jnp.repeat(heights, dims[dim] // blocks).reshape([-1 if axis == dim else 1 for axis in range(len(dims))])
    return gain


def bell_draw(own_key, dims, scale, most, cuts=(), kind=jnp.bfloat16):
    factor_of = level_of(own_key, dims, cuts, -0.22, 0.18) if cuts else 1.0
    drawn = jax.random.normal(own_key, dims, jnp.float32) * scale * factor_of
    return jnp.minimum(jnp.maximum(drawn, -most), most).astype(kind)


def setup_inputs(seed: int = 0) -> dict:
    streams_of = jax.random.split(jax.random.key(seed), 5)
    return {
        "integrals": bell_draw(streams_of[0], (OCC, V, AUX), 0.1, 0.59765625, ((0, 16),)),
        "eps_occ": jnp.clip(jax.random.uniform(streams_of[1], (OCC,), jnp.float32, -2.0, -0.5), -2.0, -0.5),
        "eps_vir": jnp.clip(jax.random.uniform(streams_of[2], (V,), jnp.float32, 0.5, 3.0), 0.5, 3.0),
        "offsets": with_ends(jax.random.randint(streams_of[3], (PAIRS,), 0, PAIRS), jax.random.fold_in(streams_of[3], 1), 0, PAIRS - 1).astype(jnp.int32),
    }


def reference(integrals, eps_occ, eps_vir, offsets):
    whole = integrals.astype(jnp.float32)

    def step(total, shift):
        partner_tiles = jnp.roll(integrals, shift, axis=0).astype(jnp.float32)
        pair = jnp.einsum("iap,ibp->iab", whole, partner_tiles)
        e_partner = jnp.roll(eps_occ, shift)
        denom = eps_vir[None, :, None] + eps_vir[None, None, :] - eps_occ[:, None, None] - e_partner[:, None, None]
        amp = (-pair / denom).astype(jnp.bfloat16).astype(jnp.float32)
        own = jnp.einsum("iab,ibp->iap", amp, partner_tiles)
        part = jnp.einsum("iab,iap->ibp", amp, whole)
        part = lax.optimization_barrier(part.astype(jnp.bfloat16)).astype(jnp.float32)
        total = total + own + jnp.roll(part, -shift, axis=0)
        return total, None

    start = jnp.zeros(integrals.shape, jnp.float32)
    gamma, unused = lax.scan(step, start, offsets)
    return gamma
```

```python
import functools

import jax
import jax.numpy as jnp
from jax import lax
from jax.experimental import pallas as pl
from jax.experimental.pallas import tpu as pltpu
from jax.sharding import PartitionSpec as P

CHUNK = 256


def exchange(block, axis, mask):
    devices = range(lax.axis_size(axis))
    return lax.ppermute(block, axis, [(i, i ^ mask) for i in devices])


def cut(block, pieces):
    rows = block.shape[0] // pieces
    return [block[i * rows : (i + 1) * rows] for i in range(pieces)]


def absorb_kernel(plan, sizes, place, table, e_occ, e_row, e_part, e_col, *refs):
    lefts_plan, blocks_plan, fresh, final = plan
    occupied, part_rows, width = sizes
    n_left, n_block = len(lefts_plan), len(blocks_plan)
    lefts, refs = refs[:n_left], refs[n_left:]
    blocks, refs = refs[:n_block], refs[n_block:]
    olds = [None] * n_left if fresh else refs[:n_left]
    news = refs[-n_left:]
    here, slot = place[0], place[1]
    entries = table.shape[0]

    rights, slices, rows, tags = [], [], [], []
    for block, (mask, piece) in zip(blocks, blocks_plan):
        rights.append(block[...])
        slices.append(block[:, pl.ds(pl.multiple_of(slot * width, width), width)])
        l = here ^ mask
        tags.append(l)
        if piece is None:
            row = e_row[...]
        else:
            r, p, pieces = piece
            row = e_part[pl.ds((slot ^ r) * pieces + p, 1), :]
        rows.append(row - e_occ[l])
    counts = [right.shape[0] for right in rights]
    right = jnp.concatenate(rights, axis=0) if len(rights) > 1 else rights[0]
    row = jnp.concatenate(rows, axis=1) if len(rows) > 1 else rows[0]

    groups = []
    start = 0
    for i, (mask, _) in enumerate(blocks_plan):
        if groups and groups[-1][0] == mask:
            groups[-1][2] += counts[i]
            groups[-1][3].append(slices[i])
        else:
            groups.append([mask, start, counts[i], [slices[i]]])
        start += counts[i]

    for left, old, new, mask_k in zip(lefts, olds, news, lefts_plan):
        k = here ^ mask_k
        weights = []
        for mask, _, _, _ in groups:
            ahead = (k - (here ^ mask)) & (occupied - 1)
            back = ((here ^ mask) - k) & (occupied - 1)
            total = jnp.int32(0)
            for n in range(entries):
                d = table[n] & (occupied - 1)
                total = total - (d == ahead).astype(jnp.int32) - (d == back).astype(jnp.int32)
            weights.append(total.astype(jnp.float32))
        for at in range(0, left.shape[0], CHUNK):
            pair = lax.dot_general(
                left[at : at + CHUNK], right, (((1,), (1,)), ((), ())),
                preferred_element_type=jnp.float32,
            )
            column = e_col[at : at + CHUNK, :1] - e_occ[k]
            amp = (pair / (column + row)).astype(jnp.bfloat16)
            total = None if old is None else old[at : at + CHUNK]
            for (_, start, count, parts), weight in zip(groups, weights):
                side = jnp.concatenate(parts, axis=0) if len(parts) > 1 else parts[0]
                term = weight * jnp.dot(
                    amp[:, start : start + count], side, preferred_element_type=jnp.float32
                )
                total = term if total is None else total + term
            new[at : at + CHUNK] = total.astype(new.dtype)


def in_vmem(array):
    return pltpu.with_memory_space_constraint(array, pltpu.VMEM)


def absorb(context, sizes, lefts, blocks, olds, final=False):
    plan = (
        tuple(mask for _, mask in lefts),
        tuple((mask, piece) for _, mask, piece in blocks),
        olds is None,
        final,
    )
    rows, width = lefts[0][0].shape[0], sizes[2]
    arrays = [in_vmem(a) for a, _ in lefts] + [in_vmem(b) for b, _, _ in blocks]
    arrays += [] if olds is None else [in_vmem(t) for t in olds]
    kind = jnp.bfloat16 if final else jnp.float32
    scalar = pl.BlockSpec(memory_space=pltpu.SMEM)
    whole = pl.BlockSpec(memory_space=pltpu.VMEM)
    n_in = len(context) + len(arrays)
    aliases = {}
    if olds is not None and not final:
        aliases = {n_in - len(lefts) + i: i for i in range(len(lefts))}
    depth = sum(b.shape[0] for b, _, _ in blocks)
    aux = lefts[0][0].shape[1]
    return pl.pallas_call(
        functools.partial(absorb_kernel, plan, sizes),
        out_shape=[pltpu.VMEM((rows, width), kind) for _ in lefts],
        in_specs=[scalar] * 3 + [whole] * (n_in - 3),
        out_specs=[whole] * len(lefts),
        input_output_aliases=aliases,
        compiler_params=pltpu.CompilerParams(vmem_limit_bytes=24 * 1024 * 1024),
        cost_estimate=pl.CostEstimate(
            flops=2 * len(lefts) * rows * depth * (aux + width),
            bytes_accessed=1024 * 1024,
            transcendentals=0,
        ),
    )(*context, *arrays)


def per_device(integrals, eps_occ, eps_vir, offsets):
    tile = integrals[0]
    virtuals, aux = tile.shape
    occupied = eps_occ.shape[0]
    reps = lax.axis_size("rep")
    lines = lax.axis_size("blk") // 4
    here = lax.axis_index("blk")
    slot = lax.axis_index("rep")
    part = virtuals // reps
    width = aux // reps
    pieces = max(1, 4 // reps)
    rows = part // pieces
    sizes = (occupied, rows, width)

    across = exchange(tile, "blk", 2)
    mine = lax.dynamic_slice_in_dim(tile, slot * part, part, axis=0)
    halves = cut(mine, pieces)
    table = offsets
    bit = 1
    while bit < reps:
        table = jnp.concatenate([table, exchange(table, "rep", bit)])
        bit *= 2

    line = {}
    for m in range(1, lines):
        for p in range(pieces):
            low = m & -m
            source = halves[p] if m == low else line[m ^ low, p]
            line[m, p] = exchange(source, "blk", 4 * low)
    twin = exchange(tile, "blk", 1)

    context = [
        jnp.stack([here, slot]).astype(jnp.int32),
        table,
        eps_occ,
        eps_vir[None, :],
        eps_vir.reshape(virtuals // rows, rows),
        jnp.broadcast_to(eps_vir[:, None], (virtuals, 128)),
    ]
    near, far = (tile, 0), (across, 2)
    first = [(tile, 0, None), (twin, 1, None)]
    (own,) = absorb(context, sizes, [near], first, None)

    steps = []
    for m in range(1, lines):
        for p in range(pieces):
            got = {0: line[m, p]}
            for r in range(1, reps):
                low = r & -r
                got[r] = exchange(got[r ^ low], "rep", low)
            blocks = [(got[r], 4 * m, (r, p, pieces)) for r in range(reps)]
            blocks += [
                (exchange(got[r], "blk", 1), 4 * m + 1, (r, p, pieces)) for r in range(reps)
            ]
            steps.append(blocks)

    (own,) = absorb(context, sizes, [near], steps[0], [own])
    (theirs,) = absorb(context, sizes, [far], first, None)
    (theirs,) = absorb(context, sizes, [far], steps[0], [theirs])
    for blocks in steps[1:-1]:
        own, theirs = absorb(context, sizes, [near, far], blocks, [own, theirs])
    (theirs,) = absorb(context, sizes, [far], steps[-1], [theirs], final=True)
    (own,) = absorb(context, sizes, [near], steps[-1], [own])
    gamma = own + exchange(theirs, "blk", 2).astype(jnp.float32)
    return gamma[None]


def solution(mesh):
    in_specs = (P("blk", None, None), P(), P(), P("rep"))
    out_specs = P("blk", None, "rep")
    return jax.shard_map(
        per_device, mesh=mesh, in_specs=in_specs, out_specs=out_specs, check_vma=False
    )
```

```python
import functools

import jax
import jax.numpy as jnp
from jax import lax
from jax.experimental import pallas as pl
from jax.experimental.pallas import tpu as pltpu
from jax.sharding import PartitionSpec as P

CHUNK = 256
MIB = 1024 * 1024


def exchange(block, axis, mask):
    devices = range(lax.axis_size(axis))
    return lax.ppermute(block, axis, [(i, i ^ mask) for i in devices])


def gate(blocks, after):
    anywhere = pl.BlockSpec(memory_space=pl.ANY)
    return pl.pallas_call(
        lambda *refs: None,
        out_shape=[jax.ShapeDtypeStruct(b.shape, b.dtype) for b in blocks],
        in_specs=[anywhere] * (len(blocks) + len(after)),
        out_specs=[anywhere] * len(blocks),
        input_output_aliases={i: i for i in range(len(blocks))},
        compiler_params=pltpu.CompilerParams(vmem_limit_bytes=MIB),
        cost_estimate=pl.CostEstimate(flops=0, bytes_accessed=0, transcendentals=0),
    )(*blocks, *after)


def absorb_kernel(plan, sizes, place, table, e_occ, e_half, e_col, *refs):
    left_masks, block_plan, fresh = plan
    occupied, width, parts = sizes
    n_left, n_block = len(left_masks), len(block_plan)
    n_total = n_left * parts
    lefts, refs = refs[:n_left], refs[n_left:]
    blocks, refs = refs[:n_block], refs[n_block:]
    olds = None if fresh else refs[:n_total]
    news = refs[-n_total:]
    here, slot = place[0], place[1]

    for i, (left, mask_k) in enumerate(zip(lefts, left_masks)):
        k = here ^ mask_k

        def weight(l):
            ahead = (k - l) & (occupied - 1)
            back = (l - k) & (occupied - 1)
            total = jnp.int32(0)
            for n in range(table.shape[0]):
                d = table[n] & (occupied - 1)
                total = total - (d == ahead).astype(jnp.int32) - (d == back).astype(jnp.int32)
            return total.astype(jnp.float32)

        for at in range(0, left.shape[0], CHUNK):
            column = e_col[at : at + CHUNK, :1] - e_occ[k]
            amps = []
            for block, runs in zip(blocks, block_plan):
                pair = lax.dot_general(
                    left[at : at + CHUNK], block[...], (((1,), (1,)), ((), ())),
                    preferred_element_type=jnp.float32,
                )
                rows = []
                for mask, first, count in runs:
                    pieces = [e_half[pl.ds(slot * 2 + first + j, 1), :] for j in range(count)]
                    rows += [piece - e_occ[here ^ mask] for piece in pieces]
                row = jnp.concatenate(rows, axis=1) if len(rows) > 1 else rows[0]
                amps.append((pair / (column + row)).astype(jnp.bfloat16))
            for q in range(parts):
                lanes = pl.ds(pl.multiple_of((slot ^ q) * width, width), width)
                total = None if fresh else olds[i * parts + q][at : at + CHUNK]
                for amp, block, runs in zip(amps, blocks, block_plan):
                    start = 0
                    for mask, _, count in runs:
                        stop = start + count * e_half.shape[1]
                        term = weight(here ^ mask) * jnp.dot(
                            amp[:, start:stop], block[start:stop, lanes],
                            preferred_element_type=jnp.float32,
                        )
                        total = term if total is None else total + term
                        start = stop
                new = news[i * parts + q]
                new[at : at + CHUNK] = total.astype(new.dtype)


def in_vmem(array):
    return pltpu.with_memory_space_constraint(array, pltpu.VMEM)


def absorb(context, sizes, lefts, blocks, olds, kinds=None):
    virtuals, aux = lefts[0][0].shape
    _, width, parts = sizes
    plan = (
        tuple(mask for _, mask in lefts),
        tuple(tuple(runs) for _, runs in blocks),
        olds is None,
    )
    n_total = len(lefts) * parts
    kinds = kinds or [jnp.float32] * n_total
    arrays = [in_vmem(a) for a, _ in lefts] + [in_vmem(b) for b, _ in blocks]
    arrays += [] if olds is None else [in_vmem(t) for t in olds]
    scalar = pl.BlockSpec(memory_space=pltpu.SMEM)
    whole = pl.BlockSpec(memory_space=pltpu.VMEM)
    n_in = len(context) + len(arrays)
    aliases = {}
    if olds is not None:
        base = n_in - n_total
        aliases = {base + i: i for i in range(n_total) if kinds[i] == jnp.float32}
    depth = sum(b.shape[0] for b, _ in blocks)
    return pl.pallas_call(
        functools.partial(absorb_kernel, plan, sizes),
        out_shape=[pltpu.VMEM((virtuals, width), kind) for kind in kinds],
        in_specs=[scalar] * 3 + [whole] * (n_in - 3),
        out_specs=[whole] * n_total,
        input_output_aliases=aliases,
        compiler_params=pltpu.CompilerParams(vmem_limit_bytes=24 * MIB),
        cost_estimate=pl.CostEstimate(
            flops=4 * len(lefts) * virtuals * depth * aux, bytes_accessed=0, transcendentals=0
        ),
    )(*context, *arrays)


def per_device(integrals, eps_occ, eps_vir, offsets):
    tile = integrals[0]
    virtuals, aux = tile.shape
    occupied = eps_occ.shape[0]
    reps = lax.axis_size("rep")
    lines = lax.axis_size("blk") // 4
    here = lax.axis_index("blk")
    slot = lax.axis_index("rep")
    part = virtuals // reps
    half = part // 2
    width = aux // reps
    sizes = (occupied, width, reps)

    mine = lax.dynamic_slice_in_dim(tile, slot * part, part, axis=0)
    line = {(0, 0): mine[:half], (0, 1): mine[half:]}
    beside = exchange(mine, "blk", 2)
    table = offsets
    bit = 1
    while bit < reps:
        table = jnp.concatenate([table, exchange(table, "rep", bit)])
        bit *= 2
    twin = exchange(tile, "blk", 1)
    lefts = [(tile, 0), (twin, 1)]
    context = [
        jnp.stack([here, slot]).astype(jnp.int32),
        table,
        eps_occ,
        eps_vir.reshape(virtuals // half, half),
        jnp.broadcast_to(eps_vir[:, None], (virtuals, 128)),
    ]
    totals = absorb(context, sizes, lefts, [(mine, [(0, 0, 2)])], None)

    steps = []
    for level in range(1, lines.bit_length()):
        members = [m for m in range(1, lines) if m.bit_count() == level]
        steps += [(members, h) for h in range(2)]
    sides = [(beside, [(2, 0, 2)]), None]
    for members, h in steps:
        for m in members:
            low = m & -m
            line[m, h] = exchange(line[m ^ low, h], "blk", 4 * low)
        blocks = gate([line[m, h] for m in members], [totals[0]])
        for m, block in zip(members, blocks):
            line[m, h] = block
        group = jnp.concatenate(blocks, axis=0) if len(blocks) > 1 else blocks[0]
        sides.append((exchange(group, "blk", 2), [(4 * m + 2, h, 1) for m in members]))
        arrived = sides.pop(0)
        blocks = [] if arrived is None else [arrived]
        blocks.append((group, [(4 * m, h, 1) for m in members]))
        totals = absorb(context, sizes, lefts, blocks, totals)
    for arrived in sides[:-1]:
        totals = absorb(context, sizes, lefts, [arrived], totals)
    last = [sides[-1]]
    kinds = [jnp.float32] + [jnp.bfloat16] * (reps - 1)
    theirs = absorb(context, sizes, lefts[1:], last, totals[reps:], kinds)
    ours = absorb(context, sizes, lefts[:1], last, totals[:reps])
    gamma = ours[0] + exchange(theirs[0], "blk", 1)
    for q in range(1, reps):
        sent = ours[q] + exchange(theirs[q], "blk", 1).astype(jnp.float32)
        gamma = gamma + exchange(sent.astype(jnp.bfloat16), "rep", q).astype(jnp.float32)
    return gamma[None]


def solution(mesh):
    in_specs = (P("blk", None, None), P(), P(), P("rep"))
    out_specs = P("blk", None, "rep")
    return jax.shard_map(
        per_device, mesh=mesh, in_specs=in_specs, out_specs=out_specs, check_vma=False
    )
```

```python
import functools

import jax
import jax.numpy as jnp
from jax import lax
from jax.experimental import pallas as pl
from jax.experimental.pallas import tpu as pltpu
from jax.sharding import PartitionSpec as P

CHUNK = 256
SPLIT = 4
MIB = 1024 * 1024


def exchange(block, axis, mask):
    devices = range(lax.axis_size(axis))
    return lax.ppermute(block, axis, [(i, i ^ mask) for i in devices])


def gate(blocks, after):
    anywhere = pl.BlockSpec(memory_space=pl.ANY)
    return pl.pallas_call(
        lambda *refs: None,
        out_shape=[jax.ShapeDtypeStruct(b.shape, b.dtype) for b in blocks],
        in_specs=[anywhere] * (len(blocks) + len(after)),
        out_specs=[anywhere] * len(blocks),
        input_output_aliases={i: i for i in range(len(blocks))},
        compiler_params=pltpu.CompilerParams(vmem_limit_bytes=MIB),
        cost_estimate=pl.CostEstimate(flops=0, bytes_accessed=0, transcendentals=0),
    )(*blocks, *after)


def join_kernel(*refs):
    out, start = refs[-1], 0
    for ref in refs[:-1]:
        out[start : start + ref.shape[0]] = ref[...]
        start += ref.shape[0]


def join(blocks):
    rows = sum(b.shape[0] for b in blocks)
    whole = pl.BlockSpec(memory_space=pltpu.VMEM)
    return pl.pallas_call(
        join_kernel,
        out_shape=pltpu.VMEM((rows, blocks[0].shape[1]), blocks[0].dtype),
        in_specs=[whole] * len(blocks),
        out_specs=whole,
        compiler_params=pltpu.CompilerParams(vmem_limit_bytes=8 * MIB),
        cost_estimate=pl.CostEstimate(flops=0, bytes_accessed=0, transcendentals=0),
    )(*[in_vmem(b) for b in blocks])


def absorb_kernel(plan, sizes, place, table, e_occ, e_half, e_col, *refs):
    left_masks, block_plan, fresh, parts = plan
    occupied, width = sizes
    n_left, n_block = len(left_masks), len(block_plan)
    n_total = n_left * len(parts)
    lefts, refs = refs[:n_left], refs[n_left:]
    blocks, refs = refs[:n_block], refs[n_block:]
    olds = None if fresh else refs[:n_total]
    news = refs[-n_total:]
    here, slot = place[0], place[1]
    half = e_half.shape[1]

    merged = []
    for block, runs in zip(blocks, block_plan):
        if merged and len(merged[-1][1]) + len(runs) <= 2:
            merged[-1][0].append(block)
            merged[-1][1].extend(runs)
        else:
            merged.append(([block], list(runs)))

    def weight(k, l):
        ahead = (k - l) & (occupied - 1)
        back = (l - k) & (occupied - 1)
        total = jnp.int32(0)
        for n in range(table.shape[0]):
            d = table[n] & (occupied - 1)
            total = total - (d == ahead).astype(jnp.int32) - (d == back).astype(jnp.int32)
        return total.astype(jnp.float32)

    masks = {mask for runs in block_plan for mask, _, _ in runs}
    weights = [{m: weight(here ^ k, here ^ m) for m in sorted(masks)} for k in left_masks]

    def amplitudes(i, at):
        column = e_col[at : at + CHUNK, :1] - e_occ[here ^ left_masks[i]]
        groups = {}
        for members, runs in merged:
            block = [member[...] for member in members]
            block = jnp.concatenate(block, axis=0) if len(block) > 1 else block[0]
            pair = lax.dot_general(
                lefts[i][at : at + CHUNK], block, (((1,), (1,)), ((), ())),
                preferred_element_type=jnp.float32,
            )
            rows = [
                e_half[pl.ds((slot ^ r) * 2 + h, 1), :] - e_occ[here ^ mask] for mask, r, h in runs
            ]
            row = jnp.concatenate(rows, axis=1) if len(rows) > 1 else rows[0]
            amp = (pair / (column + row)).astype(jnp.bfloat16)
            places = [(b, s) for b in members for s in range(0, b.shape[0], half)]
            for n, ((mask, _, _), place) in enumerate(zip(runs, places)):
                groups.setdefault(mask, []).append((amp[:, n * half : (n + 1) * half], *place))
        return groups

    tasks = [(i, at) for i in range(n_left) for at in range(0, lefts[0].shape[0], CHUNK)]
    ready = [amplitudes(*task) for task in tasks]
    for (i, at), groups in zip(tasks, ready):
        for j, q in enumerate(parts):
            lanes = pl.ds(pl.multiple_of((slot ^ q) * width, width), width)
            total = None if fresh else olds[i * len(parts) + j][at : at + CHUNK]
            for mask, members in groups.items():
                amps = [amp for amp, _, _ in members]
                sides = [block[s : s + half, lanes] for _, block, s in members]
                term = weights[i][mask] * jnp.dot(
                    jnp.concatenate(amps, axis=1) if len(amps) > 1 else amps[0],
                    jnp.concatenate(sides, axis=0) if len(sides) > 1 else sides[0],
                    preferred_element_type=jnp.float32,
                )
                total = term if total is None else total + term
            news[i * len(parts) + j][at : at + CHUNK] = total


def in_vmem(array):
    return pltpu.with_memory_space_constraint(array, pltpu.VMEM)


def absorb(context, width, lefts, blocks, parts, olds, cost):
    virtuals, aux = lefts[0][0].shape
    keys = [(mask, q) for _, mask in lefts for q in parts]
    fresh = keys[0] not in olds
    plan = (tuple(m for _, m in lefts), tuple(tuple(r) for _, r in blocks), fresh, tuple(parts))
    sizes = (context[2].shape[0], width)
    arrays = [in_vmem(a) for a, _ in lefts] + [in_vmem(b) for b, _ in blocks]
    base = len(context) + len(arrays)
    arrays += [] if fresh else [in_vmem(olds[key]) for key in keys]
    scalar = pl.BlockSpec(memory_space=pltpu.SMEM)
    whole = pl.BlockSpec(memory_space=pltpu.VMEM)
    depth = sum(b.shape[0] for b, _ in blocks)
    news = pl.pallas_call(
        functools.partial(absorb_kernel, plan, sizes),
        out_shape=[pltpu.VMEM((virtuals, width), jnp.float32) for _ in keys],
        in_specs=[scalar] * 3 + [whole] * (len(context) - 3 + len(arrays)),
        out_specs=[whole] * len(keys),
        input_output_aliases={} if fresh else {base + i: i for i in range(len(keys))},
        compiler_params=pltpu.CompilerParams(vmem_limit_bytes=24 * MIB),
        cost_estimate=pl.CostEstimate(
            flops=cost * 2 * len(lefts) * virtuals * depth * (aux + width * len(parts)),
            bytes_accessed=0, transcendentals=0,
        ),
    )(*context, *arrays)
    return {**olds, **dict(zip(keys, news))}


def across(total, pieces):
    return jnp.concatenate([exchange(t, "blk", 1) for t in jnp.split(total, pieces)])


def per_device(integrals, eps_occ, eps_vir, offsets):
    tile = integrals[0]
    virtuals, aux = tile.shape
    reps = lax.axis_size("rep")
    lines = lax.axis_size("blk") // 4
    here = lax.axis_index("blk")
    slot = lax.axis_index("rep")
    part = virtuals // reps
    half = part // 2
    width = aux // reps
    every = list(range(reps))
    rest = every[1:]

    mine = lax.dynamic_slice_in_dim(tile, slot * part, part, axis=0)
    line = {(0, 0): mine[:half], (0, 1): mine[half:]}
    side = {}
    beside = exchange(mine, "blk", 2)
    table = offsets
    bit = 1
    while bit < reps:
        table = jnp.concatenate([table, exchange(table, "rep", bit)])
        bit *= 2
    twin = exchange(tile, "blk", 1)
    own, other = (tile, 0), (twin, 1)
    context = [
        jnp.stack([here, slot]).astype(jnp.int32),
        table,
        eps_occ,
        eps_vir.reshape(2 * reps, half),
        jnp.broadcast_to(eps_vir[:, None], (virtuals, 128)),
    ]

    def add(blocks, totals, parts=every, lefts=(own, other), cost=0):
        return absorb(context, width, lefts, blocks, parts, totals, cost)

    def travel(members, h, after):
        for m in members:
            low = m & -m
            line[m, h] = exchange(line[m ^ low, h], "blk", 4 * low)
        for m, block in zip(members, gate([line[m, h] for m in members], after)):
            line[m, h] = block

    def lines_of(m, h):
        return (line[m, h], [(4 * m, 0, h)])

    def sides_of(m, h):
        return (side[m, h], [(4 * m + 2, 0, h)])

    levels = [[m for m in range(1, lines) if m.bit_count() == n] for n in range(1, lines.bit_length())]
    singles, final = levels[0], lines - 1
    others = [m for level in levels[1:] for m in level]
    by = final & -final
    totals = add([(mine, [(0, 0, 0), (0, 0, 1)])], {})
    travel(singles, 0, [beside, totals[0, 0]])
    group = join([line[m, 0] for m in singles])
    group_side = exchange(group, "blk", 2)
    (line[0, 1],) = gate([line[0, 1]], [twin])
    totals = add([(beside, [(2, 0, 0), (2, 0, 1)])], totals)
    travel(singles, 1, [totals[0, 0]])
    for m in singles[::-1]:
        side[m, 1] = exchange(line[m, 1], "blk", 2)
    blocks = [(group, [(4 * m, 0, 0) for m in singles])] + [lines_of(m, 1) for m in singles]
    late = []
    for m in others:
        travel([m], 0, [line[singles[0], 1]])
        side[m, 0] = exchange(line[m, 0], "blk", 2)
        late.append(lines_of(m, 0))
        if m != final:
            travel([m], 1, [])
            side[m, 1] = exchange(line[m, 1], "blk", 2)
            late.append(lines_of(m, 1))
    totals = add(blocks, totals)
    line[final, 1] = exchange(line[final ^ by, 1], "blk", 4 * by)
    (passed,) = gate([side[final ^ by, 1]], [totals[0, 0]])
    side[final ^ by, 1] = passed
    side[final, 1] = exchange(passed, "blk", 4 * by)
    (group_side,) = gate([group_side], [passed])
    totals = add(late + [(group_side, [(4 * m + 2, 0, 0) for m in singles])], totals)
    blocks = [lines_of(final, 1)] + [sides_of(m, 1) for m in singles[::-1]]
    totals = add(blocks, totals)
    blocks = [sides_of(m, h) for m, h in side if m not in singles]

    came = []
    if rest:
        theirs = add(blocks, totals, rest, [other])
        ours = add(blocks, totals, rest, [own])
        sent = [(ours[0, q] + across(theirs[1, q], 1)).astype(jnp.bfloat16) for q in rest]
        came = [exchange(s, "rep", q) for s, q in zip(sent, rest)]
        held = gate([block for block, _ in blocks], sent)
        blocks = [(block, runs) for block, (_, runs) in zip(held, blocks)]
    totals = add(blocks, totals, [0], cost=0)
    gamma = totals[0, 0] + across(totals[1, 0], SPLIT)
    for c in came:
        gamma = gamma + c.astype(jnp.float32)
    return gamma[None]


def solution(mesh):
    in_specs = (P("blk", None, None), P(), P(), P("rep"))
    out_specs = P("blk", None, "rep")
    return jax.shard_map(
        per_device, mesh=mesh, in_specs=in_specs, out_specs=out_specs, check_vma=False
    )
```

```python
import functools

import jax
import jax.numpy as jnp
from jax import lax
from jax.experimental import pallas as pl
from jax.experimental.pallas import tpu as pltpu
from jax.sharding import PartitionSpec as P

CHUNK = 256
MIB = 1024 * 1024


def exchange(block, axis, mask):
    devices = range(lax.axis_size(axis))
    return lax.ppermute(block, axis, [(i, i ^ mask) for i in devices])


def gate(blocks, after):
    anywhere = pl.BlockSpec(memory_space=pl.ANY)
    return pl.pallas_call(
        lambda *refs: None,
        out_shape=[jax.ShapeDtypeStruct(b.shape, b.dtype) for b in blocks],
        in_specs=[anywhere] * (len(blocks) + len(after)),
        out_specs=[anywhere] * len(blocks),
        input_output_aliases={i: i for i in range(len(blocks))},
        compiler_params=pltpu.CompilerParams(vmem_limit_bytes=MIB),
        cost_estimate=pl.CostEstimate(flops=0, bytes_accessed=0, transcendentals=0),
    )(*blocks, *after)


def pieces_kernel(tile, whole, first, second, sems):
    half = first.shape[0]
    start = pl.multiple_of(lax.axis_index("rep") * (2 * half), 2 * half)
    copies = [
        pltpu.make_async_copy(tile.at[pl.ds(start, half)], first, sems.at[0]),
        pltpu.make_async_copy(tile.at[pl.ds(start + half, half)], second, sems.at[1]),
        pltpu.make_async_copy(tile.at[pl.ds(start, 2 * half)], whole, sems.at[2]),
    ]
    for copy in copies:
        copy.start()
    for copy in copies:
        copy.wait()


def pieces_of(tile, part):
    columns = tile.shape[1]
    return pl.pallas_call(
        pieces_kernel,
        out_shape=[pltpu.VMEM((n, columns), tile.dtype) for n in (part, part // 2, part // 2)],
        in_specs=[pl.BlockSpec(memory_space=pl.ANY)],
        out_specs=[pl.BlockSpec(memory_space=pltpu.VMEM)] * 3,
        scratch_shapes=[pltpu.SemaphoreType.DMA((3,))],
        compiler_params=pltpu.CompilerParams(vmem_limit_bytes=8 * MIB),
        cost_estimate=pl.CostEstimate(flops=0, bytes_accessed=0, transcendentals=0),
    )(tile)


def join_kernel(*refs):
    out, start = refs[-1], 0
    for ref in refs[:-1]:
        out[start : start + ref.shape[0]] = ref[...]
        start += ref.shape[0]


def join(blocks):
    rows = sum(b.shape[0] for b in blocks)
    whole = pl.BlockSpec(memory_space=pltpu.VMEM)
    return pl.pallas_call(
        join_kernel,
        out_shape=pltpu.VMEM((rows, blocks[0].shape[1]), blocks[0].dtype),
        in_specs=[whole] * len(blocks),
        out_specs=whole,
        compiler_params=pltpu.CompilerParams(vmem_limit_bytes=8 * MIB),
        cost_estimate=pl.CostEstimate(flops=0, bytes_accessed=0, transcendentals=0),
    )(*[in_vmem(b) for b in blocks])


def absorb_kernel(plan, sizes, place, table, e_occ, e_half, e_col, *refs):
    left_masks, block_plan, given, parts, n_addends = plan
    occupied, width = sizes
    n_left, n_block = len(left_masks), len(block_plan)
    n_total = n_left * len(parts)
    lefts, refs = refs[:n_left], refs[n_left:]
    blocks, refs = refs[:n_block], refs[n_block:]
    olds, at_old = [], 0
    for is_given in given:
        olds.append(refs[at_old] if is_given else None)
        at_old += is_given
    addends = refs[at_old : at_old + n_addends]
    news = refs[-n_total:]
    here, slot = place[0], place[1]
    half = e_half.shape[1]

    merged = []
    for block, runs in zip(blocks, block_plan):
        if merged and len(merged[-1][1]) + len(runs) <= 2:
            merged[-1][0].append(block)
            merged[-1][1].extend(runs)
        else:
            merged.append(([block], list(runs)))

    def weight(k, l):
        ahead = (k - l) & (occupied - 1)
        back = (l - k) & (occupied - 1)
        total = jnp.int32(0)
        for n in range(table.shape[0]):
            d = table[n] & (occupied - 1)
            total = total - (d == ahead).astype(jnp.int32) - (d == back).astype(jnp.int32)
        return total.astype(jnp.float32)

    masks = {mask for runs in block_plan for mask, _, _ in runs}
    weights = [{m: weight(here ^ k, here ^ m) for m in sorted(masks)} for k in left_masks]

    def amplitudes(i, at):
        column = e_col[at : at + CHUNK, :1] - e_occ[here ^ left_masks[i]]
        groups = {}
        for members, runs in merged:
            block = [member[...] for member in members]
            block = jnp.concatenate(block, axis=0) if len(block) > 1 else block[0]
            pair = lax.dot_general(
                lefts[i][at : at + CHUNK], block, (((1,), (1,)), ((), ())),
                preferred_element_type=jnp.float32,
            )
            rows = [
                e_half[pl.ds(((slot ^ r) if r >= 0 else ~r) * 2 + h, 1), :] - e_occ[here ^ mask]
                for mask, r, h in runs
            ]
            row = jnp.concatenate(rows, axis=1) if len(rows) > 1 else rows[0]
            amp = (pair / (column + row)).astype(jnp.bfloat16)
            places = [(b, s) for b in members for s in range(0, b.shape[0], half)]
            for n, ((mask, _, _), place) in enumerate(zip(runs, places)):
                groups.setdefault(mask, []).append((amp[:, n * half : (n + 1) * half], *place))
        return groups

    tasks = [(i, at) for i in range(n_left) for at in range(0, lefts[0].shape[0], CHUNK)]
    ready = [amplitudes(*task) for task in tasks]
    for (i, at), groups in zip(tasks, ready):
        for j, q in enumerate(parts):
            lanes = pl.ds(pl.multiple_of((slot ^ q) * width, width), width)
            n = i * len(parts) + j
            total = None if olds[n] is None else olds[n][at : at + CHUNK]
            for mask, members in groups.items():
                amps = [amp for amp, _, _ in members]
                sides = [block[s : s + half, lanes] for _, block, s in members]
                term = weights[i][mask] * jnp.dot(
                    jnp.concatenate(amps, axis=1) if len(amps) > 1 else amps[0],
                    jnp.concatenate(sides, axis=0) if len(sides) > 1 else sides[0],
                    preferred_element_type=jnp.float32,
                )
                total = term if total is None else total + term
            if addends:
                total = total + addends[n][at : at + CHUNK]
            news[n][at : at + CHUNK] = total.astype(news[n].dtype)


def in_vmem(array):
    return pltpu.with_memory_space_constraint(array, pltpu.VMEM)


def absorb(context, width, lefts, blocks, parts, olds, cost, addends=(), kind=jnp.float32):
    virtuals, aux = lefts[0][0].shape
    keys = [(mask, q) for _, mask in lefts for q in parts]
    given = tuple(key in olds for key in keys)
    plan = (
        tuple(m for _, m in lefts), tuple(tuple(r) for _, r in blocks), given, tuple(parts), len(addends)
    )
    sizes = (context[2].shape[0], width)
    arrays = [in_vmem(a) for a, _ in lefts] + [in_vmem(b) for b, _ in blocks]
    base = len(context) + len(arrays)
    arrays += [in_vmem(olds[key]) for key in keys if key in olds] + [in_vmem(a) for a in addends]
    aliases = {}
    for i, is_given in enumerate(given):
        if is_given and kind == jnp.float32:
            aliases[base + sum(given[:i])] = i
    scalar = pl.BlockSpec(memory_space=pltpu.SMEM)
    whole = pl.BlockSpec(memory_space=pltpu.VMEM)
    depth = sum(b.shape[0] for b, _ in blocks)
    news = pl.pallas_call(
        functools.partial(absorb_kernel, plan, sizes),
        out_shape=[pltpu.VMEM((virtuals, width), kind) for _ in keys],
        in_specs=[scalar] * 3 + [whole] * (len(context) - 3 + len(arrays)),
        out_specs=[whole] * len(keys),
        input_output_aliases=aliases,
        compiler_params=pltpu.CompilerParams(vmem_limit_bytes=24 * MIB),
        cost_estimate=pl.CostEstimate(
            flops=cost * 2 * len(lefts) * virtuals * depth * (aux + width * len(parts)),
            bytes_accessed=0, transcendentals=0,
        ),
    )(*context, *arrays)
    return {**olds, **dict(zip(keys, news))}


def across(total, pieces):
    return jnp.concatenate([exchange(t, "blk", 1) for t in jnp.split(total, pieces)])


def per_device(integrals, eps_occ, eps_vir, offsets):
    tile = integrals[0]
    virtuals, aux = tile.shape
    reps = lax.axis_size("rep")
    lines = lax.axis_size("blk") // 4
    here = lax.axis_index("blk")
    slot = lax.axis_index("rep")
    part = virtuals // reps
    half = part // 2
    width = aux // reps
    every = list(range(reps))
    rest = every[1:]

    mine, *halves = pieces_of(tile, part)
    line = {(0, h): halves[h] for h in range(2)}
    side = {}
    twin = exchange(tile, "blk", 1)
    (mine,) = gate([mine], [twin])
    beside = exchange(mine, "blk", 2)
    table = offsets
    bit = 1
    while bit < reps:
        table = jnp.concatenate([table, exchange(table, "rep", bit)])
        bit *= 2
    own, other = (tile, 0), (twin, 1)
    context = [
        jnp.stack([here, slot]).astype(jnp.int32),
        table,
        eps_occ,
        eps_vir.reshape(2 * reps, half),
        jnp.broadcast_to(eps_vir[:, None], (virtuals, 128)),
    ]

    def add(blocks, totals, parts=every, lefts=(own, other), **options):
        return absorb(context, width, lefts, blocks, parts, totals, options.pop('cost', 0), **options)

    def travel(members, h, after):
        for m in members:
            low = m & -m
            line[m, h] = exchange(line[m ^ low, h], "blk", 4 * low)
        for m, block in zip(members, gate([line[m, h] for m in members], after)):
            line[m, h] = block

    def lines_of(m, h):
        return (line[m, h], [(4 * m, 0, h)])

    def sides_of(m, h):
        return (side[m, h], [(4 * m + 2, 0, h)])

    levels = [[m for m in range(1, lines) if m.bit_count() == n] for n in range(1, lines.bit_length())]
    singles, final = levels[0][::-1], lines - 1
    others = [m for level in levels[1:] for m in level]
    by = final & -final
    totals = add([(tile, [(0, ~r, h) for r in every for h in range(2)])], {}, [0], cost=1)
    travel(singles, 0, [totals[0, 0]])
    for m in singles:
        side[m, 0] = exchange(line[m, 0], "blk", 2)
    (line[0, 1],) = gate([line[0, 1]], [twin])
    totals = add([(beside, [(2, 0, 0), (2, 0, 1)])], totals, cost=1)
    travel(singles, 1, [totals[0, 0]])
    for m in singles:
        side[m, 1] = exchange(line[m, 1], "blk", 2)
    blocks = [lines_of(m, h) for m in singles for h in range(2)]
    blocks += [sides_of(m, 0) for m in singles]
    totals = add(blocks, totals, cost=1)
    late = []
    for m in others:
        travel([m], 0, [totals[0, 0]])
        side[m, 0] = exchange(line[m, 0], "blk", 2)
        late.append(lines_of(m, 0))
        if m != final:
            travel([m], 1, [])
            side[m, 1] = exchange(line[m, 1], "blk", 2)
            late.append(lines_of(m, 1))
    line[final, 1] = exchange(line[final ^ by, 1], "blk", 4 * by)
    (passed,) = gate([side[final ^ by, 1]], [totals[0, 0]])
    side[final ^ by, 1] = passed
    side[final, 1] = exchange(passed, "blk", 4 * by)
    (line[final, 1],) = gate([line[final, 1]], [passed])
    blocks = late + [lines_of(final, 1)] + [sides_of(m, 1) for m in singles]
    totals = add(blocks, totals)
    blocks = [sides_of(m, h) for m, h in side if m not in singles]
    came = []
    if rest:
        theirs = add(blocks, totals, rest, [other], kind=jnp.bfloat16)
        ours = add(blocks, totals, rest, [own])
        for q in rest:
            sent = ours[0, q] + exchange(theirs[1, q], "blk", 1).astype(jnp.float32)
            sent = sent.astype(jnp.bfloat16)
            came.append(exchange(sent, "rep", q))
        held = gate([block for block, _ in blocks], [sent])
        blocks = [(block, runs) for block, (_, runs) in zip(held, blocks)]
    totals = add(blocks, totals, [0])
    gamma = totals[0, 0] + across(totals[1, 0], 4)
    for c in came:
        gamma = gamma + c.astype(jnp.float32)
    return gamma[None]


def solution(mesh):
    in_specs = (P("blk", None, None), P(), P(), P("rep"))
    out_specs = P("blk", None, "rep")
    return jax.shard_map(
        per_device, mesh=mesh, in_specs=in_specs, out_specs=out_specs, check_vma=False
    )
```

```python
import functools

import jax
import jax.numpy as jnp
from jax import lax
from jax.experimental import pallas as pl
from jax.experimental.pallas import tpu as pltpu
from jax.sharding import PartitionSpec as P

CHUNK = 256
MIB = 1024 * 1024


def exchange(block, axis, mask):
    devices = range(lax.axis_size(axis))
    return lax.ppermute(block, axis, [(i, i ^ mask) for i in devices])


def gate(blocks, after):
    anywhere = pl.BlockSpec(memory_space=pl.ANY)
    return pl.pallas_call(
        lambda *refs: None,
        out_shape=[jax.ShapeDtypeStruct(b.shape, b.dtype) for b in blocks],
        in_specs=[anywhere] * (len(blocks) + len(after)),
        out_specs=[anywhere] * len(blocks),
        input_output_aliases={i: i for i in range(len(blocks))},
        compiler_params=pltpu.CompilerParams(vmem_limit_bytes=MIB),
        cost_estimate=pl.CostEstimate(flops=0, bytes_accessed=0, transcendentals=0),
    )(*blocks, *after)


def pieces_kernel(tile, whole, first, second, sems):
    half = first.shape[0]
    start = pl.multiple_of(lax.axis_index("rep") * (2 * half), 2 * half)
    copies = [
        pltpu.make_async_copy(tile.at[pl.ds(start, half)], first, sems.at[0]),
        pltpu.make_async_copy(tile.at[pl.ds(start + half, half)], second, sems.at[1]),
        pltpu.make_async_copy(tile.at[pl.ds(start, 2 * half)], whole, sems.at[2]),
    ]
    for copy in copies:
        copy.start()
    for copy in copies:
        copy.wait()


def pieces_of(tile, part):
    columns = tile.shape[1]
    return pl.pallas_call(
        pieces_kernel,
        out_shape=[pltpu.VMEM((n, columns), tile.dtype) for n in (part, part // 2, part // 2)],
        in_specs=[pl.BlockSpec(memory_space=pl.ANY)],
        out_specs=[pl.BlockSpec(memory_space=pltpu.VMEM)] * 3,
        scratch_shapes=[pltpu.SemaphoreType.DMA((3,))],
        compiler_params=pltpu.CompilerParams(vmem_limit_bytes=8 * MIB),
        cost_estimate=pl.CostEstimate(flops=0, bytes_accessed=0, transcendentals=0),
    )(tile)


def absorb_kernel(plan, sizes, place, table, e_occ, e_half, e_col, *refs):
    left_masks, block_plan, given, parts = plan
    occupied, width = sizes
    n_left, n_block = len(left_masks), len(block_plan)
    n_total = n_left * len(parts)
    lefts, refs = refs[:n_left], refs[n_left:]
    blocks, refs = refs[:n_block], refs[n_block:]
    olds, at_old = [], 0
    for is_given in given:
        olds.append(refs[at_old] if is_given else None)
        at_old += is_given
    news = refs[-n_total:]
    here, slot = place[0], place[1]
    half = e_half.shape[1]

    merged = []
    for block, runs in zip(blocks, block_plan):
        if merged and len(merged[-1][1]) + len(runs) <= 2:
            merged[-1][0].append(block)
            merged[-1][1].extend(runs)
        else:
            merged.append(([block], list(runs)))

    def weight(k, l):
        ahead = (k - l) & (occupied - 1)
        back = (l - k) & (occupied - 1)
        total = jnp.int32(0)
        for n in range(table.shape[0]):
            d = table[n] & (occupied - 1)
            total = total - (d == ahead).astype(jnp.int32) - (d == back).astype(jnp.int32)
        return total.astype(jnp.float32)

    masks = {mask for runs in block_plan for mask, _, _ in runs}
    weights = [{m: weight(here ^ k, here ^ m) for m in sorted(masks)} for k in left_masks]

    def amplitudes(i, at):
        column = e_col[at : at + CHUNK, :1] - e_occ[here ^ left_masks[i]]
        groups = {}
        for members, runs in merged:
            block = [member[...] for member in members]
            block = jnp.concatenate(block, axis=0) if len(block) > 1 else block[0]
            pair = lax.dot_general(
                lefts[i][at : at + CHUNK], block, (((1,), (1,)), ((), ())),
                preferred_element_type=jnp.float32,
            )
            rows = [
                e_half[pl.ds(((slot ^ r) if r >= 0 else ~r) * 2 + h, 1), :] - e_occ[here ^ mask]
                for mask, r, h in runs
            ]
            row = jnp.concatenate(rows, axis=1) if len(rows) > 1 else rows[0]
            amp = (pair / (column + row)).astype(jnp.bfloat16)
            places = [(b, s) for b in members for s in range(0, b.shape[0], half)]
            for n, ((mask, _, _), place) in enumerate(zip(runs, places)):
                groups.setdefault(mask, []).append((amp[:, n * half : (n + 1) * half], *place))
        return groups

    tasks = [(i, at) for i in range(n_left) for at in range(0, lefts[0].shape[0], CHUNK)]
    ready = [amplitudes(*task) for task in tasks]
    for (i, at), groups in zip(tasks, ready):
        for j, q in enumerate(parts):
            lanes = pl.ds(pl.multiple_of((slot ^ q) * width, width), width)
            n = i * len(parts) + j
            total = None if olds[n] is None else olds[n][at : at + CHUNK]
            for mask, members in groups.items():
                amps = [amp for amp, _, _ in members]
                sides = [block[s : s + half, lanes] for _, block, s in members]
                term = weights[i][mask] * jnp.dot(
                    jnp.concatenate(amps, axis=1) if len(amps) > 1 else amps[0],
                    jnp.concatenate(sides, axis=0) if len(sides) > 1 else sides[0],
                    preferred_element_type=jnp.float32,
                )
                total = term if total is None else total + term
            news[n][at : at + CHUNK] = total.astype(news[n].dtype)


def in_vmem(array):
    return pltpu.with_memory_space_constraint(array, pltpu.VMEM)


def absorb(context, width, lefts, blocks, parts, olds, cost=0, kind=jnp.float32):
    virtuals, aux = lefts[0][0].shape
    keys = [(mask, q) for _, mask in lefts for q in parts]
    given = tuple(key in olds for key in keys)
    plan = (
        tuple(m for _, m in lefts), tuple(tuple(r) for _, r in blocks), given, tuple(parts)
    )
    sizes = (context[2].shape[0], width)
    arrays = [in_vmem(a) for a, _ in lefts] + [in_vmem(b) for b, _ in blocks]
    base = len(context) + len(arrays)
    arrays += [in_vmem(olds[key]) for key in keys if key in olds]
    aliases = {}
    for i, is_given in enumerate(given):
        if is_given and kind == jnp.float32:
            aliases[base + sum(given[:i])] = i
    scalar = pl.BlockSpec(memory_space=pltpu.SMEM)
    whole = pl.BlockSpec(memory_space=pltpu.VMEM)
    depth = sum(b.shape[0] for b, _ in blocks)
    news = pl.pallas_call(
        functools.partial(absorb_kernel, plan, sizes),
        out_shape=[pltpu.VMEM((virtuals, width), kind) for _ in keys],
        in_specs=[scalar] * 3 + [whole] * (len(context) - 3 + len(arrays)),
        out_specs=[whole] * len(keys),
        input_output_aliases=aliases,
        compiler_params=pltpu.CompilerParams(vmem_limit_bytes=24 * MIB),
        cost_estimate=pl.CostEstimate(
            flops=cost * 2 * len(lefts) * virtuals * depth * (aux + width * len(parts)),
            bytes_accessed=0, transcendentals=0,
        ),
    )(*context, *arrays)
    return {**olds, **dict(zip(keys, news))}


def across(total, pieces):
    return jnp.concatenate([exchange(t, "blk", 1) for t in jnp.split(total, pieces)])


def per_device(integrals, eps_occ, eps_vir, offsets):
    tile = integrals[0]
    virtuals, aux = tile.shape
    reps = lax.axis_size("rep")
    lines = lax.axis_size("blk") // 4
    here = lax.axis_index("blk")
    slot = lax.axis_index("rep")
    part = virtuals // reps
    half = part // 2
    width = aux // reps
    every = list(range(reps))
    rest = every[1:]

    mine, *halves = pieces_of(tile, part)
    line = {(0, h): halves[h] for h in range(2)}
    side = {}
    twin = exchange(tile, "blk", 1)
    (mine,) = gate([mine], [twin])
    beside = exchange(mine, "blk", 2)
    table = offsets
    bit = 1
    while bit < reps:
        table = jnp.concatenate([table, exchange(table, "rep", bit)])
        bit *= 2
    own, other = (tile, 0), (twin, 1)
    context = [
        jnp.stack([here, slot]).astype(jnp.int32),
        table,
        eps_occ,
        eps_vir.reshape(2 * reps, half),
        jnp.broadcast_to(eps_vir[:, None], (virtuals, 128)),
    ]

    def add(blocks, totals, parts=every, lefts=(own, other), **options):
        return absorb(context, width, lefts, blocks, parts, totals, **options)

    def travel(members, h, after):
        for m in members:
            low = m & -m
            line[m, h] = exchange(line[m ^ low, h], "blk", 4 * low)
        for m, block in zip(members, gate([line[m, h] for m in members], after)):
            line[m, h] = block

    def lines_of(m, h):
        return (line[m, h], [(4 * m, 0, h)])

    def sides_of(m, h):
        return (side[m, h], [(4 * m + 2, 0, h)])

    levels = [[m for m in range(1, lines) if m.bit_count() == n] for n in range(1, lines.bit_length())]
    singles, final = levels[0][::-1], lines - 1
    others = [m for level in levels[1:] for m in level]
    by = final & -final
    totals = add([(tile, [(0, ~r, h) for r in every for h in range(2)])], {}, [0], cost=1)
    travel(singles, 0, [twin])
    for m in singles:
        side[m, 0] = exchange(line[m, 0], "blk", 2)
    (line[0, 1],) = gate([line[0, 1]], [twin])
    totals = add([(beside, [(2, 0, 0), (2, 0, 1)])], totals, cost=1)
    after = [totals[0, 0]]
    for m in singles:
        travel([m], 1, after)
        side[m, 1] = exchange(line[m, 1], "blk", 2)
        after = [line[m, 1]]
    blocks = [lines_of(m, h) for m in singles for h in range(2)]
    blocks += [sides_of(m, 0) for m in singles]
    totals = add(blocks, totals, cost=1)
    late = []
    for m in others:
        travel([m], 0, [totals[0, 0]])
        side[m, 0] = exchange(line[m, 0], "blk", 2)
        late.append(lines_of(m, 0))
        if m != final:
            travel([m], 1, [])
            side[m, 1] = exchange(line[m, 1], "blk", 2)
            late.append(lines_of(m, 1))
    line[final, 1] = exchange(line[final ^ by, 1], "blk", 4 * by)
    (passed,) = gate([side[final ^ by, 1]], [totals[0, 0]])
    side[final ^ by, 1] = passed
    side[final, 1] = exchange(passed, "blk", 4 * by)
    (line[final, 1],) = gate([line[final, 1]], [passed])
    blocks = late + [lines_of(final, 1)] + [sides_of(m, 1) for m in singles]
    totals = add(blocks, totals)
    blocks = [sides_of(m, h) for m, h in side if m not in singles]
    came = []
    if rest:
        theirs = add(blocks, totals, rest, [other], kind=jnp.bfloat16)
        ours = add(blocks, totals, rest, [own])
        for q in rest:
            sent = ours[0, q] + exchange(theirs[1, q], "blk", 1).astype(jnp.float32)
            sent = sent.astype(jnp.bfloat16)
            came.append(exchange(sent, "rep", q))
        held = gate([block for block, _ in blocks], [sent])
        blocks = [(block, runs) for block, (_, runs) in zip(held, blocks)]
    totals = add(blocks, totals, [0])
    gamma = totals[0, 0] + across(totals[1, 0], 4)
    for c in came:
        gamma = gamma + c.astype(jnp.float32)
    return gamma[None]


def solution(mesh):
    in_specs = (P("blk", None, None), P(), P(), P("rep"))
    out_specs = P("blk", None, "rep")
    return jax.shard_map(
        per_device, mesh=mesh, in_specs=in_specs, out_specs=out_specs, check_vma=False
    )
```
